32 devices in a mesh: seg: 2 (over y), gx: 8 (over z, x), gy: 2 (over core).
Axes of the slice: x: 2, y: 2, z: 4, core: 2. Of those that a mesh axis runs over, the one named last changes fastest.
Arguments:
- populations: float32 [52, 64, 64, 128], P('seg', 'gx', 'gy'), parts along dimension 0, may hold values from 0 to 1, as said below
- cell_flags: int32 [64, 64, 256], P('gx', 'gy', 'seg'), parts along dimension 2, may hold values from 0 to 3, as said below
Outputs:
- fields: float32 [10, 64, 64, 128], P('seg', 'gx', 'gy'), parts along dimension 0
The draws below stay inside these ranges and needn't reach their ends.
There are 2 independent parts, one for each index of `seg`. The reference program is written for one: setup_inputs(seed, part) draws one part's arguments, and reference() takes and returns one part's arrays. A program takes and returns all parts, laid end to end along the dimension named above; each array names one. Nothing has to cross between parts.
Inputs may be any that keep to these rules, and one draw needn't show every extreme that they name: `populations`: populations are positive and near a local equilibrium of each cell. `cell_flags`: the value 2 is added only on the first and last plane along the channel height.
All inputs are finite; a program needn't handle non-finite values.
Results may differ from the reference program's by a relative error of at most 0.0001.
Values sent between devices are 32-bit elements; how exact they have to be, the bound alone decides.
A program may use at most 64 MiB of HBM per device.

```python
import jax
import jax.numpy as jnp
from jax import lax

NZ = 128
STEPS = 3
NX = 64
NY = 64


VELOCITY = [(0, 0, 0), (1, 0, 0), (-1, 0, 0), (0, 1, 0), (0, -1, 0), (0, 0, 1), (0, 0, -1), (1, 1, 0), (-1, -1, 0), (1, -1, 0), (-1, 1, 0), (1, 0, 1), (-1, 0, -1), (1, 0, -1), (-1, 0, 1), (0, 1, 1), (0, -1, -1), (0, 1, -1), (0, -1, 1)]


FLOW_WEIGHT = [1.0 / 3.0] + [1.0 / 18.0] * 6 + [1.0 / 36.0] * 12


SALT_WEIGHT = [0.25] + [0.125] * 6


def draw_populations(key, part):
    key = jax.random.fold_in(key, 11)
    keys = jax.random.split(key, 6)
    shape = (NX, NY, NZ)
    density = 1.0 + 0.03 * jnp.clip(jax.random.normal(keys[0], shape, jnp.float32), -2.5, 2.5)
    speeds = [0.06 * jnp.clip(jax.random.normal(keys[1 + a], shape, jnp.float32), -2.5, 2.5) for a in range(3)]
    conc = jax.random.uniform(keys[4], shape, jnp.float32, 0.5, 1.5)
    usq = speeds[0] * speeds[0] + speeds[1] * speeds[1] + speeds[2] * speeds[2]
    pieces = []
    for q in range(26):
        vec = VELOCITY[q] if q < 19 else VELOCITY[q - 19]
        along = vec[0] * speeds[0] + vec[1] * speeds[1] + vec[2] * speeds[2]
        jitter = 1.0 + 0.05 * jnp.clip(jax.random.normal(jax.random.fold_in(keys[5], q), shape, jnp.float32), -3.0, 3.0)
        if q < 19:
            base = FLOW_WEIGHT[q] * density * (1.0 + 3.0 * along + 4.5 * along * along - 1.5 * usq)
        else:
            base = SALT_WEIGHT[q - 19] * conc * (1.0 + 4.0 * along)
        pieces.append(base * jitter)
    return jnp.stack(pieces).astype(jnp.float32)


def draw_cell_flags(key, part):
    key = jax.random.fold_in(key, 23)
    first, second = jax.random.split(key)
    shape = (NX, NY, NZ)
    solid = (jax.random.randint(first, shape, 0, 6) == 0).astype(jnp.int32)
    permeable = (jax.random.randint(second, shape, 0, 4) != 0).astype(jnp.int32)
    height = lax.broadcasted_iota(jnp.int32, shape, 2)
    wall = ((height == 0) | (height == NZ - 1)).astype(jnp.int32)
    return (solid + 2 * permeable * wall).astype(jnp.int32)


def setup_inputs(seed: int = 0, part: int = 0) -> dict:
    streams_of = jax.random.split(jax.random.key(seed), 3)
    part_splits = jax.random.split(jax.random.fold_in(streams_of[2], part), 3)
    populations = draw_populations(jax.random.fold_in(jax.random.fold_in(streams_of[2], part), 71), part)
    cell_flags = draw_cell_flags(jax.random.fold_in(jax.random.fold_in(streams_of[2], part), 71), part)
    return dict(populations=populations, cell_flags=cell_flags)


VELOCITY = [(0, 0, 0), (1, 0, 0), (-1, 0, 0), (0, 1, 0), (0, -1, 0), (0, 0, 1), (0, 0, -1),
            (1, 1, 0), (-1, -1, 0), (1, -1, 0), (-1, 1, 0), (1, 0, 1), (-1, 0, -1),
            (1, 0, -1), (-1, 0, 1), (0, 1, 1), (0, -1, -1), (0, 1, -1), (0, -1, 1)]
FLOW_WEIGHT = [1.0 / 3.0] + [1.0 / 18.0] * 6 + [1.0 / 36.0] * 12
SALT_WEIGHT = [0.25] + [0.125] * 6
tau_plus = 0.65
tau_minus = 0.5 + 0.25 / (tau_plus - 0.5)
salt_minus = 0.7
salt_plus = 0.5 + 0.25 / (salt_minus - 0.5)
speed_scale = 0.1


def partner(index):
    if index == 0:
        return 0
    return index + 1 if index % 2 == 1 else index - 1


def lattice_vector(index):
    return VELOCITY[index] if index < 19 else VELOCITY[index - 19]


def opposite_of(index):
    return partner(index) if index < 19 else 19 + partner(index - 19)


def component(pops, first, axis):
    total = None
    for offset in range(len(pops)):
        sign = lattice_vector(first + offset)[axis]
        if sign != 0:
            term = pops[offset] if sign > 0 else -pops[offset]
            total = term if total is None else total + term
    return total


def collide(state, flags):
    solid_mask = (flags % 2) == 1
    open_wall = (flags // 2).astype(jnp.float32) * (1.0 - solid_mask.astype(jnp.float32))
    flow = [state[q] for q in range(19)]
    salt = [state[19 + k] for k in range(7)]
    density = sum(flow[1:], flow[0])
    speeds = [component(flow, 0, a) / density for a in range(3)]
    usq = speeds[0] * speeds[0] + speeds[1] * speeds[1] + speeds[2] * speeds[2]
    post = [None] * 26
    post[0] = flow[0] - (flow[0] - density * (1.0 - 1.5 * usq) / 3.0) / tau_plus
    for q in range(1, 19, 2):
        other = q + 1
        vec = VELOCITY[q]
        along = vec[0] * speeds[0] + vec[1] * speeds[1] + vec[2] * speeds[2]
        weight = FLOW_WEIGHT[q]
        even_eq = weight * density * (1.0 + 4.5 * along * along - 1.5 * usq)
        odd_eq = 3.0 * weight * density * along
        dplus = (0.5 * (flow[q] + flow[other]) - even_eq) / tau_plus
        dminus = (0.5 * (flow[q] - flow[other]) - odd_eq) / tau_minus
        post[q] = flow[q] - dplus - dminus
        post[other] = flow[other] - dplus + dminus
    conc = sum(salt[1:], salt[0])
    post[19] = salt[0] - (salt[0] - 0.25 * conc) / salt_plus
    for k in range(1, 7, 2):
        other = k + 1
        vec = VELOCITY[k]
        along = vec[0] * speeds[0] + vec[1] * speeds[1] + vec[2] * speeds[2]
        weight = SALT_WEIGHT[k]
        even_eq = weight * conc
        odd_eq = 4.0 * weight * conc * along
        dplus = (0.5 * (salt[k] + salt[other]) - even_eq) / salt_plus
        dminus = (0.5 * (salt[k] - salt[other]) - odd_eq) / salt_minus
        post[19 + k] = salt[k] - dplus - dminus
        post[19 + other] = salt[other] - dplus + dminus
    post = [jnp.where(solid_mask, state[opposite_of(q)], post[q]) for q in range(26)]
    rate = 0.03 * (1.5 - 0.5 * conc) * open_wall
    flow_loss = 6.0 * density * rate
    salt_loss = 0.02 * conc * open_wall
    return jnp.stack(post), flow_loss, salt_loss


def slide_xy(extended):
    span_x = extended.shape[1] - 2
    span_y = extended.shape[2] - 2
    moved = []
    for q in range(26):
        vec = lattice_vector(q)
        moved.append(extended[q, 1 - vec[0]:1 - vec[0] + span_x, 1 - vec[1]:1 - vec[1] + span_y])
    return moved


def finish(moved, inner, flow_loss, salt_loss):
    parts = []
    for q in range(26):
        rise = lattice_vector(q)[2]
        source = moved[q]
        if rise == 0:
            parts.append(source)
            continue
        loss = flow_loss * FLOW_WEIGHT[q] if q < 19 else salt_loss
        if rise == 1:
            entering = inner[opposite_of(q)][:, :, :1] - loss[:, :, :1]
            parts.append(jnp.concatenate([entering, source[:, :, :-1]], axis=2))
        else:
            entering = inner[opposite_of(q)][:, :, -1:] - loss[:, :, -1:]
            parts.append(jnp.concatenate([source[:, :, 1:], entering], axis=2))
    return jnp.stack(parts)


def moments(state):
    flow = [state[q] for q in range(19)]
    salt = [state[19 + k] for k in range(7)]
    density = sum(flow[1:], flow[0])
    momenta = [component(flow, 0, a) / speed_scale for a in range(3)]
    conc = sum(salt[1:], salt[0])
    return jnp.stack([density] + momenta + [conc])


def reference(populations, cell_flags):
    state = populations
    for step in range(STEPS):
        post, flow_loss, salt_loss = collide(state, cell_flags)
        extended = jnp.pad(post, ((0, 0), (1, 1), (1, 1), (0, 0)), mode="wrap")
        state = finish(slide_xy(extended), post, flow_loss, salt_loss)
    return moments(state)
```

```python
import functools

import jax
import jax.numpy as jnp
from jax import lax
from jax.experimental import pallas as pl
from jax.experimental.pallas import tpu as pltpu
from jax.sharding import PartitionSpec as P

MESH = pl.DeviceIdType.MESH
STEPS = 3

VELOCITY = [
    (0, 0, 0),
    (1, 0, 0),
    (-1, 0, 0),
    (0, 1, 0),
    (0, -1, 0),
    (0, 0, 1),
    (0, 0, -1),
    (1, 1, 0),
    (-1, -1, 0),
    (1, -1, 0),
    (-1, 1, 0),
    (1, 0, 1),
    (-1, 0, -1),
    (1, 0, -1),
    (-1, 0, 1),
    (0, 1, 1),
    (0, -1, -1),
    (0, 1, -1),
    (0, -1, 1),
]
VECTORS = VELOCITY + VELOCITY[:7]
FLOW_WEIGHT = [1.0 / 3.0] + [1.0 / 18.0] * 6 + [1.0 / 36.0] * 12
tau_plus = 0.65
tau_minus = 0.5 + 0.25 / (tau_plus - 0.5)
salt_minus = 0.7
salt_plus = 0.5 + 0.25 / (salt_minus - 0.5)
speed_scale = 0.1

ORDER = [9, 1, 11, 13, 20, 7, 3, 15, 17, 22, 10, 2, 12, 14, 21, 8, 4, 16, 18, 23]
ORDER += [0, 5, 6, 19, 24, 25]
SLOT = [ORDER.index(q) for q in range(26)]
SLANTED = [(11, 12), (14, 13), (15, 16), (18, 17)]
ROW = 8


def collide(f, flags):
    solid = (flags & 1) == 1
    open_wall = jnp.where(solid, 0.0, (flags >> 1).astype(jnp.float32))
    both = {q: f[q] + f[q + 1] for q in (*range(1, 19, 2), 20, 22, 24)}
    diff = {q: f[q] - f[q + 1] for q in (*range(1, 19, 2), 20, 22, 24)}
    density = f[0] + (
        ((both[1] + both[3]) + (both[5] + both[7]))
        + ((both[9] + both[11]) + (both[13] + both[15]))
        + both[17]
    )
    flux = [
        (diff[1] + diff[7]) + (diff[9] + diff[11]) + diff[13],
        (diff[3] + diff[7]) + (diff[15] + diff[17]) - diff[9],
        (diff[5] + diff[11]) + (diff[15] - diff[13]) - diff[17],
    ]
    inverse = 1.0 / density
    speed = [j * inverse for j in flux]
    rest = density - 1.5 * (flux[0] * speed[0] + flux[1] * speed[1] + flux[2] * speed[2])
    scaled = [4.5 * u for u in speed]

    def along(vec, values):
        total = None
        for sign, value in zip(vec, values):
            if sign == 0:
                continue
            if total is None:
                total = value
            else:
                total = total + value if sign > 0 else total - value
        return total

    post = [None] * 26
    post[0] = f[0] * (1.0 - 1.0 / tau_plus) + rest * (1.0 / (3.0 * tau_plus))
    for q in range(1, 19, 2):
        vec, weight = VELOCITY[q], FLOW_WEIGHT[q]
        j = along(vec, flux)
        even = j * along(vec, scaled) + rest
        dplus = both[q] * (0.5 / tau_plus) - even * (weight / tau_plus)
        dminus = diff[q] * (0.5 / tau_minus) - j * (3.0 * weight / tau_minus)
        post[q] = (f[q] - dplus) - dminus
        post[q + 1] = (f[q + 1] - dplus) + dminus
    conc = f[19] + ((both[20] + both[22]) + both[24])
    post[19] = f[19] * (1.0 - 1.0 / salt_plus) + conc * (0.25 / salt_plus)
    even = conc * (0.125 / salt_plus)
    for a in range(3):
        q = 20 + 2 * a
        dplus = both[q] * (0.5 / salt_plus) - even
        dminus = (diff[q] - conc * speed[a]) * (0.5 / salt_minus)
        post[q] = (f[q] - dplus) - dminus
        post[q + 1] = (f[q + 1] - dplus) + dminus
    for first in (*range(1, 19, 2), 20, 22, 24):
        post[first] = jnp.where(solid, f[first + 1], post[first])
        post[first + 1] = jnp.where(solid, f[first], post[first + 1])
    post[0] = jnp.where(solid, f[0], post[0])
    post[19] = jnp.where(solid, f[19], post[19])
    flow_loss = density * ((0.27 - 0.09 * conc) * open_wall)
    salt_loss = (0.02 * conc) * open_wall
    return post, flow_loss, salt_loss


def kernel(
    sizes, pops, flags, out, state, flag, fields, post, enter, load_sem, out_sem, send_sem, recv_sem
):
    nx, ny = sizes
    n_tiles = ny // 8
    nz = state.shape[-1]
    last = nx - 1
    inner_rows, below, above = pl.ds(ROW, ny), ROW - 1, ROW + ny

    size_x, size_y = lax.axis_size("gx"), lax.axis_size("gy")
    gx, gy = lax.axis_index("gx"), lax.axis_index("gy")
    right, left = lax.rem(gx + 1, size_x), lax.rem(gx + size_x - 1, size_x)
    other = lax.rem(gy + 1, size_y)

    def load(i, x, n):
        return pltpu.make_async_copy(
            pops.at[:, pl.ds(x, n)], state.at[:, pl.ds(x, n)], load_sem.at[i]
        )

    flag_load = pltpu.make_async_copy(flags, flag, load_sem.at[3])
    loads = [load(0, 0, 1), load(1, last, 1), load(2, 1, nx - 2)]
    flag_load.start()
    for item in loads:
        item.start()

    barrier = pltpu.get_barrier_semaphore()
    partners = [(left, gy), (right, gy), (gx, other), (left, other), (right, other)]
    for px, py in partners:
        pl.semaphore_signal(
            barrier, inc=1, device_id={"gx": px, "gy": py}, device_id_type=MESH
        )

    lane = lax.broadcasted_iota(jnp.int32, (8, nz), 1)
    floor, ceiling = lane == 0, lane == nz - 1

    def copies(s):
        buf = post.at[s]

        def copy(i, src, dst, px, py):
            return pltpu.make_async_remote_copy(
                src_ref=buf.at[src],
                dst_ref=buf.at[dst],
                send_sem=send_sem.at[s, i],
                recv_sem=recv_sem.at[s, i],
                device_id={"gx": px, "gy": py},
                device_id_type=MESH,
            )

        def at(q, n, x, nxs, row, rows=1):
            return (pl.ds(SLOT[q], n), pl.ds(x, nxs), pl.ds(row, rows))

        top = ROW + ny - 1
        to_left = [
            copy(0, at(10, 6, 1, 1, ROW, ny), at(10, 6, nx + 1, 1, ROW, ny), left, gy),
            copy(1, at(10, 1, 1, 1, top), at(10, 1, nx + 1, 1, below), left, other),
            copy(2, at(8, 1, 1, 1, ROW), at(8, 1, nx + 1, 1, above), left, other),
        ]
        to_right = [
            copy(3, at(9, 6, nx, 1, ROW, ny), at(9, 6, 0, 1, ROW, ny), right, gy),
            copy(4, at(7, 1, nx, 1, top), at(7, 1, 0, 1, below), right, other),
            copy(5, at(9, 1, nx, 1, ROW), at(9, 1, 0, 1, above), right, other),
        ]
        to_other = [
            copy(6, at(7, 6, 1, nx, top), at(7, 6, 1, nx, below), gx, other),
            copy(7, at(8, 5, 1, nx, ROW), at(8, 5, 1, nx, above), gx, other),
            copy(8, at(9, 1, 1, nx, ROW), at(9, 1, 1, nx, above), gx, other),
        ]
        return to_left, to_right, to_other

    exchange = [copies(s) for s in range(STEPS)]

    def pull(s, x, t):
        f = []
        for q in range(26):
            ex, ey, ez = VECTORS[q]
            f.append(post[s, SLOT[q], x + (1 - ex), pl.ds(ROW + 8 * t - ey, 8), :])
        for i, (rising, falling) in enumerate(SLANTED):
            wall = enter[s, i, x, pl.ds(8 * t, 8), :]
            f[rising] = jnp.where(floor, wall, f[rising])
            f[falling] = jnp.where(ceiling, wall, f[falling])
        return f

    def advance(s, x, t):
        rows = pl.ds(8 * t, 8)
        if s == 0:
            f = [state[q, x, rows, :] for q in range(26)]
        else:
            f = pull(s - 1, x, t)
        new, flow_loss, salt_loss = collide(f, flag[x, rows, :])

        def up(value):
            return pltpu.roll(value, 1, 1)

        def down(value):
            return pltpu.roll(value, nz - 1, 1)

        for i, (rising, falling) in enumerate(SLANTED):
            wall = jnp.where(floor, new[falling], new[rising])
            enter[s, i, x, rows, :] = wall - FLOW_WEIGHT[rising] * flow_loss
            new[rising], new[falling] = up(new[rising]), down(new[falling])
        for rising, falling, loss in ((5, 6, FLOW_WEIGHT[5] * flow_loss), (24, 25, salt_loss)):
            low, high = new[falling] - loss, new[rising] - loss
            new[rising] = jnp.where(floor, low, up(new[rising]))
            new[falling] = jnp.where(ceiling, high, down(new[falling]))
        for q in range(26):
            post[s, SLOT[q], x + 1, pl.ds(ROW + 8 * t, 8), :] = new[q]

    def measure(x, t):
        f = pull(STEPS - 1, x, t)
        rows = pl.ds(8 * t, 8)
        fields[0, x, rows, :] = sum(f[1:19], f[0])
        for a in range(3):
            total = None
            for q in range(1, 19, 2):
                sign = VELOCITY[q][a]
                if sign:
                    term = f[q] - f[q + 1]
                    if total is None:
                        total = term if sign > 0 else -term
                    else:
                        total = total + term if sign > 0 else total - term
            fields[1 + a, x, rows, :] = total * (1.0 / speed_scale)
        fields[4, x, rows, :] = sum(f[20:], f[19])

    def planes(work, lo, hi, tiles):
        def body(x, carry):
            for t in tiles:
                work(x, t)
            return carry

        lax.fori_loop(lo, hi, body, 0)

    every = range(n_tiles)
    middle = range(1, n_tiles - 1)
    edge = (0, n_tiles - 1)

    work = functools.partial(advance, 0)
    flag_load.wait()
    loads[0].wait()
    planes(work, 0, 1, every)
    pl.semaphore_wait(barrier, len(partners))
    for item in exchange[0][0]:
        item.start()
    loads[1].wait()
    planes(work, last, nx, every)
    for item in exchange[0][1]:
        item.start()
    loads[2].wait()
    planes(work, 1, last, every)
    for item in exchange[0][2]:
        item.start()

    for s in range(1, STEPS + 1):
        work = functools.partial(advance, s) if s < STEPS else measure
        to_left, to_right, to_other = exchange[s - 1]
        planes(work, 1, last, middle)
        for item in to_other:
            item.wait_recv()
        planes(work, 1, last, edge)
        if s == STEPS:
            part = pl.ds(1, nx - 2)
            stores = [pltpu.make_async_copy(fields.at[:, part], out.at[:, part], out_sem.at[0])]
            stores[0].start()
        for item in to_right:
            item.wait_recv()
        planes(work, 0, 1, every)
        if s < STEPS:
            for item in exchange[s][0]:
                item.start()
        else:
            part = pl.ds(0, 1)
            stores.append(
                pltpu.make_async_copy(fields.at[:, part], out.at[:, part], out_sem.at[1])
            )
            stores[1].start()
        for item in to_left:
            item.wait_recv()
        planes(work, last, nx, every)
        if s < STEPS:
            for item in exchange[s][1] + exchange[s][2]:
                item.start()
        else:
            part = pl.ds(last, 1)
            stores.append(
                pltpu.make_async_copy(fields.at[:, part], out.at[:, part], out_sem.at[2])
            )
            stores[2].start()

    for group in exchange:
        for side in group:
            for item in side:
                item.wait_send()
    for item in stores:
        item.wait()


def per_device(populations, cell_flags):
    _, nx, ny, nz = populations.shape
    return pl.pallas_call(
        functools.partial(kernel, (nx, ny)),
        out_shape=jax.ShapeDtypeStruct((5, nx, ny, nz), jnp.float32),
        in_specs=[pl.BlockSpec(memory_space=pl.ANY)] * 2,
        out_specs=pl.BlockSpec(memory_space=pl.ANY),
        scratch_shapes=[
            pltpu.VMEM((26, nx, ny, nz), jnp.float32),
            pltpu.VMEM((nx, ny, nz), jnp.int32),
            pltpu.VMEM((5, nx, ny, nz), jnp.float32),
            pltpu.VMEM((STEPS, 26, nx + 2, ny + 2 * ROW, nz), jnp.float32),
            pltpu.VMEM((STEPS, 4, nx, ny, nz), jnp.float32),
            pltpu.SemaphoreType.DMA((4,)),
            pltpu.SemaphoreType.DMA((3,)),
            pltpu.SemaphoreType.DMA((STEPS, 9)),
            pltpu.SemaphoreType.DMA((STEPS, 9)),
        ],
        compiler_params=pltpu.CompilerParams(
            collective_id=0, has_side_effects=True, vmem_limit_bytes=52 * 2**20
        ),
        cost_estimate=pl.CostEstimate(
            flops=900 * nx * ny * nz, bytes_accessed=128 * nx * ny * nz, transcendentals=0
        ),
    )(populations, cell_flags)


def solution(mesh):
    return jax.shard_map(
        per_device,
        mesh=mesh,
        in_specs=(P("seg", "gx", "gy", None), P("gx", "gy", "seg")),
        out_specs=P("seg", "gx", "gy", None),
        check_vma=False,
    )
```

```python
import functools

import jax
import jax.numpy as jnp
from jax import lax
from jax.experimental import pallas as pl
from jax.experimental.pallas import tpu as pltpu
from jax.sharding import PartitionSpec as P

MESH = pl.DeviceIdType.MESH
STEPS = 3

VELOCITY = [
    (0, 0, 0),
    (1, 0, 0),
    (-1, 0, 0),
    (0, 1, 0),
    (0, -1, 0),
    (0, 0, 1),
    (0, 0, -1),
    (1, 1, 0),
    (-1, -1, 0),
    (1, -1, 0),
    (-1, 1, 0),
    (1, 0, 1),
    (-1, 0, -1),
    (1, 0, -1),
    (-1, 0, 1),
    (0, 1, 1),
    (0, -1, -1),
    (0, 1, -1),
    (0, -1, 1),
]
VECTORS = VELOCITY + VELOCITY[:7]
FLOW_WEIGHT = [1.0 / 3.0] + [1.0 / 18.0] * 6 + [1.0 / 36.0] * 12
tau_plus = 0.65
tau_minus = 0.5 + 0.25 / (tau_plus - 0.5)
salt_minus = 0.7
salt_plus = 0.5 + 0.25 / (salt_minus - 0.5)
speed_scale = 0.1

ORDER = [9, 1, 11, 13, 20, 7, 3, 15, 17, 22, 10, 2, 12, 14, 21, 8, 4, 16, 18, 23]
ORDER += [0, 5, 6, 19, 24, 25]
SLOT = [ORDER.index(q) for q in range(26)]
SLANTED = [(11, 12), (14, 13), (15, 16), (18, 17)]
ROW = 8


def collide(f, flags):
    solid = (flags & 1) == 1
    open_wall = jnp.where(solid, 0.0, (flags >> 1).astype(jnp.float32))
    both = {q: f[q] + f[q + 1] for q in (*range(1, 19, 2), 20, 22, 24)}
    diff = {q: f[q] - f[q + 1] for q in (*range(1, 19, 2), 20, 22, 24)}
    density = f[0] + (
        ((both[1] + both[3]) + (both[5] + both[7]))
        + ((both[9] + both[11]) + (both[13] + both[15]))
        + both[17]
    )
    flux = [
        (diff[1] + diff[7]) + (diff[9] + diff[11]) + diff[13],
        (diff[3] + diff[7]) + (diff[15] + diff[17]) - diff[9],
        (diff[5] + diff[11]) + (diff[15] - diff[13]) - diff[17],
    ]
    inverse = 1.0 / density
    speed = [j * inverse for j in flux]
    rest = density - 1.5 * (flux[0] * speed[0] + flux[1] * speed[1] + flux[2] * speed[2])
    scaled = [4.5 * u for u in speed]

    def along(vec, values):
        total = None
        for sign, value in zip(vec, values):
            if sign == 0:
                continue
            if total is None:
                total = value
            else:
                total = total + value if sign > 0 else total - value
        return total

    post = [None] * 26
    post[0] = f[0] * (1.0 - 1.0 / tau_plus) + rest * (1.0 / (3.0 * tau_plus))
    for q in range(1, 19, 2):
        vec, weight = VELOCITY[q], FLOW_WEIGHT[q]
        j = along(vec, flux)
        even = j * along(vec, scaled) + rest
        dplus = both[q] * (0.5 / tau_plus) - even * (weight / tau_plus)
        dminus = diff[q] * (0.5 / tau_minus) - j * (3.0 * weight / tau_minus)
        post[q] = (f[q] - dplus) - dminus
        post[q + 1] = (f[q + 1] - dplus) + dminus
    conc = f[19] + ((both[20] + both[22]) + both[24])
    post[19] = f[19] * (1.0 - 1.0 / salt_plus) + conc * (0.25 / salt_plus)
    even = conc * (0.125 / salt_plus)
    for a in range(3):
        q = 20 + 2 * a
        dplus = both[q] * (0.5 / salt_plus) - even
        dminus = (diff[q] - conc * speed[a]) * (0.5 / salt_minus)
        post[q] = (f[q] - dplus) - dminus
        post[q + 1] = (f[q + 1] - dplus) + dminus
    for first in (*range(1, 19, 2), 20, 22, 24):
        post[first] = jnp.where(solid, f[first + 1], post[first])
        post[first + 1] = jnp.where(solid, f[first], post[first + 1])
    post[0] = jnp.where(solid, f[0], post[0])
    post[19] = jnp.where(solid, f[19], post[19])
    flow_loss = density * ((0.27 - 0.09 * conc) * open_wall)
    salt_loss = (0.02 * conc) * open_wall
    return post, flow_loss, salt_loss


def kernel(
    sizes, pops, flags, out, state, flag, fields, post, enter, load_sem, out_sem, send_sem, recv_sem
):
    nx, ny = sizes
    n_tiles = ny // 8
    nz = state.shape[-1]
    last = nx - 1
    below, above = ROW - 1, ROW + ny

    size_x, size_y = lax.axis_size("gx"), lax.axis_size("gy")
    gx, gy = lax.axis_index("gx"), lax.axis_index("gy")
    odd = lax.rem(gx, 2)
    far = lax.rem(gx + size_x - 1 + 2 * odd, size_x)
    near = lax.rem(gx + 1 + size_x - 2 * odd, size_x)
    other = lax.rem(gy + 1, size_y)
    far_x, near_x = odd * last, (1 - odd) * last

    def tile(k):
        return k + gy * (n_tiles - 1 - 2 * k)

    def load(i, x, n):
        return pltpu.make_async_copy(
            pops.at[:, pl.ds(x, n)], state.at[:, pl.ds(x, n)], load_sem.at[i]
        )

    flag_load = pltpu.make_async_copy(flags, flag, load_sem.at[3])
    loads = [load(0, far_x, 1), load(1, near_x, 1), load(2, 1, nx - 2)]
    flag_load.start()
    for item in loads:
        item.start()

    barrier = pltpu.get_barrier_semaphore()
    partners = [(far, gy), (near, gy), (gx, other), (far, other), (near, other)]
    for px, py in partners:
        pl.semaphore_signal(
            barrier, inc=1, device_id={"gx": px, "gy": py}, device_id_type=MESH
        )

    lane = lax.broadcasted_iota(jnp.int32, (8, nz), 1)
    floor, ceiling = lane == 0, lane == nz - 1

    def copies(s):
        buf = post.at[s]

        def copy(i, src, dst, px, py):
            return pltpu.make_async_remote_copy(
                src_ref=buf.at[src],
                dst_ref=buf.at[dst],
                send_sem=send_sem.at[s, i],
                recv_sem=recv_sem.at[s, i],
                device_id={"gx": px, "gy": py},
                device_id_type=MESH,
            )

        def at(slot, n, x, nxs, row, rows=1):
            return (pl.ds(slot, n), pl.ds(x, nxs), pl.ds(row, rows))

        top = ROW + ny - 1

        def side(i, positive, x, there):
            group, halo = 10 - 10 * positive, (1 - positive) * (nx + 1)
            up, down = group + 5 * positive, group + 5 * (1 - positive)
            first, final = gy * up + (1 - gy) * down, gy * down + (1 - gy) * up
            begin, end = ROW + gy * (ny - 1), ROW + (1 - gy) * (ny - 1)
            beyond, before = ROW + ny - gy * (ny + 1), ROW - 1 + gy * (ny + 1)
            parts = []
            for k in range(n_tiles):
                row = pl.multiple_of(ROW + 8 * tile(k), 8)
                parts.append(
                    copy(i + k, at(group, 6, x + 1, 1, row, 8), at(group, 6, halo, 1, row, 8), there, gy)
                )
            i += n_tiles
            corners = [
                copy(i, at(first, 1, x + 1, 1, begin), at(first, 1, halo, 1, beyond), there, other),
                copy(i + 1, at(final, 1, x + 1, 1, end), at(final, 1, halo, 1, before), there, other),
            ]
            return parts, corners

        n_side = n_tiles + 2
        to_far = side(0, odd, far_x, far)
        to_near = side(n_side, 1 - odd, near_x, near)
        i = 2 * n_side
        to_other = [
            copy(i, at(5, 6, 1, nx, top), at(5, 6, 1, nx, below), gx, other),
            copy(i + 1, at(15, 5, 1, nx, ROW), at(15, 5, 1, nx, above), gx, other),
            copy(i + 2, at(0, 1, 1, nx, ROW), at(0, 1, 1, nx, above), gx, other),
        ]
        return to_far, to_near, to_other

    exchange = [copies(s) for s in range(STEPS)]

    def tile_rows(t):
        return pl.ds(pl.multiple_of(8 * t, 8), 8)

    def pull(s, x, t):
        f = []
        for q in range(26):
            ex, ey, ez = VECTORS[q]
            f.append(post[s, SLOT[q], x + (1 - ex), pl.ds(8 * t + (ROW - ey), 8), :])
        for i, (rising, falling) in enumerate(SLANTED):
            wall = enter[s, i, x, tile_rows(t), :]
            f[rising] = jnp.where(floor, wall, f[rising])
            f[falling] = jnp.where(ceiling, wall, f[falling])
        return f

    def advance(s, x, t):
        rows = tile_rows(t)
        if s == 0:
            f = [state[q, x, rows, :] for q in range(26)]
        else:
            f = pull(s - 1, x, t)
        new, flow_loss, salt_loss = collide(f, flag[x, rows, :])

        def up(value):
            return pltpu.roll(value, 1, 1)

        def down(value):
            return pltpu.roll(value, nz - 1, 1)

        for i, (rising, falling) in enumerate(SLANTED):
            wall = jnp.where(floor, new[falling], new[rising])
            enter[s, i, x, rows, :] = wall - FLOW_WEIGHT[rising] * flow_loss
            new[rising], new[falling] = up(new[rising]), down(new[falling])
        for rising, falling, loss in ((5, 6, FLOW_WEIGHT[5] * flow_loss), (24, 25, salt_loss)):
            low, high = new[falling] - loss, new[rising] - loss
            new[rising] = jnp.where(floor, low, up(new[rising]))
            new[falling] = jnp.where(ceiling, high, down(new[falling]))
        for q in range(26):
            post[s, SLOT[q], x + 1, pl.ds(pl.multiple_of(ROW + 8 * t, 8), 8), :] = new[q]

    def measure(x, t):
        f = pull(STEPS - 1, x, t)
        rows = tile_rows(t)
        fields[0, x, rows, :] = sum(f[1:19], f[0])
        for a in range(3):
            total = None
            for q in range(1, 19, 2):
                sign = VELOCITY[q][a]
                if sign:
                    term = f[q] - f[q + 1]
                    if total is None:
                        total = term if sign > 0 else -term
                    else:
                        total = total + term if sign > 0 else total - term
            fields[1 + a, x, rows, :] = total * (1.0 / speed_scale)
        fields[4, x, rows, :] = sum(f[20:], f[19])

    def planes(work, lo, hi, tiles):
        def body(x, carry):
            for t in tiles:
                work(x, t)
            return carry

        lax.fori_loop(lo, hi, body, 0)

    every = range(n_tiles)
    middle = range(1, n_tiles - 1)
    edge = (0, n_tiles - 1)

    def start(items):
        for item in items:
            item.start()

    def arrive(items):
        for item in items:
            item.wait_recv()

    def send(side, k):
        parts, corners = side
        if k == 0:
            corners[0].start()
        parts[k].start()
        if k == n_tiles - 1:
            corners[1].start()

    def receive(side, k):
        parts, corners = side
        if k == 0:
            arrive([corners[0], parts[0]])
        if k + 1 < n_tiles:
            arrive([parts[k + 1]])
        else:
            arrive([corners[1]])

    def store(i, x, n):
        item = pltpu.make_async_copy(
            fields.at[:, pl.ds(x, n)], out.at[:, pl.ds(x, n)], out_sem.at[i]
        )
        item.start()
        return item

    work = functools.partial(advance, 0)
    flag_load.wait()
    loads[0].wait()
    for k in every:
        work(far_x, tile(k))
        if k == 0:
            pl.semaphore_wait(barrier, len(partners))
        send(exchange[0][0], k)
    loads[1].wait()
    for k in every:
        work(near_x, tile(k))
        send(exchange[0][1], k)
    loads[2].wait()
    planes(work, 1, last, every)
    start(exchange[0][2])

    for s in range(1, STEPS):
        work = functools.partial(advance, s)
        to_far, to_near, to_other = exchange[s - 1]
        planes(work, 1, last, middle)
        arrive(to_other)
        planes(work, 1, last, edge)
        for k in every:
            receive(to_near, k)
            work(near_x, tile(k))
            send(exchange[s][1], k)
            receive(to_far, k)
            work(far_x, tile(k))
            send(exchange[s][0], k)
        start(exchange[s][2])

    to_far, to_near, to_other = exchange[STEPS - 1]
    planes(measure, 1, last, middle)
    arrive(to_other)
    planes(measure, 1, last, edge)
    stores = [store(0, 1, nx - 2)]
    for k in every:
        receive(to_near, k)
        measure(near_x, tile(k))
    stores.append(store(1, near_x, 1))
    for k in every:
        receive(to_far, k)
        measure(far_x, tile(k))
    stores.append(store(2, far_x, 1))

    for to_far, to_near, to_other in exchange:
        for item in (*to_far[0], *to_far[1], *to_near[0], *to_near[1], *to_other):
            item.wait_send()
    for item in stores:
        item.wait()


def per_device(populations, cell_flags):
    _, nx, ny, nz = populations.shape
    return pl.pallas_call(
        functools.partial(kernel, (nx, ny)),
        out_shape=jax.ShapeDtypeStruct((5, nx, ny, nz), jnp.float32),
        in_specs=[pl.BlockSpec(memory_space=pltpu.HBM)] * 2,
        out_specs=pl.BlockSpec(memory_space=pltpu.HBM),
        scratch_shapes=[
            pltpu.VMEM((26, nx, ny, nz), jnp.float32),
            pltpu.VMEM((nx, ny, nz), jnp.int32),
            pltpu.VMEM((5, nx, ny, nz), jnp.float32),
            pltpu.VMEM((STEPS, 26, nx + 2, ny + 2 * ROW, nz), jnp.float32),
            pltpu.VMEM((STEPS, 4, nx, ny, nz), jnp.float32),
            pltpu.SemaphoreType.DMA((4,)),
            pltpu.SemaphoreType.DMA((3,)),
            pltpu.SemaphoreType.DMA((STEPS, 2 * (ny // 8 + 2) + 3)),
            pltpu.SemaphoreType.DMA((STEPS, 2 * (ny // 8 + 2) + 3)),
        ],
        compiler_params=pltpu.CompilerParams(
            collective_id=0, has_side_effects=True, vmem_limit_bytes=52 * 2**20
        ),
        cost_estimate=pl.CostEstimate(
            flops=900 * nx * ny * nz, bytes_accessed=128 * nx * ny * nz, transcendentals=0
        ),
    )(populations, pltpu.with_memory_space_constraint(cell_flags, pltpu.HBM))


def solution(mesh):
    return jax.shard_map(
        per_device,
        mesh=mesh,
        in_specs=(P("seg", "gx", "gy", None), P("gx", "gy", "seg")),
        out_specs=P("seg", "gx", "gy", None),
        check_vma=False,
    )
```

```python
import functools

import jax
import jax.numpy as jnp
from jax import lax
from jax.experimental import pallas as pl
from jax.experimental.pallas import tpu as pltpu
from jax.sharding import PartitionSpec as P

MESH = pl.DeviceIdType.MESH
STEPS = 3

VELOCITY = [
    (0, 0, 0),
    (1, 0, 0),
    (-1, 0, 0),
    (0, 1, 0),
    (0, -1, 0),
    (0, 0, 1),
    (0, 0, -1),
    (1, 1, 0),
    (-1, -1, 0),
    (1, -1, 0),
    (-1, 1, 0),
    (1, 0, 1),
    (-1, 0, -1),
    (1, 0, -1),
    (-1, 0, 1),
    (0, 1, 1),
    (0, -1, -1),
    (0, 1, -1),
    (0, -1, 1),
]
VECTORS = VELOCITY + VELOCITY[:7]
FLOW_WEIGHT = [1.0 / 3.0] + [1.0 / 18.0] * 6 + [1.0 / 36.0] * 12
tau_plus = 0.65
tau_minus = 0.5 + 0.25 / (tau_plus - 0.5)
salt_minus = 0.7
salt_plus = 0.5 + 0.25 / (salt_minus - 0.5)
speed_scale = 0.1

ORDER = [9, 1, 11, 13, 20, 7, 3, 15, 17, 22, 10, 2, 12, 14, 21, 8, 4, 16, 18, 23]
ORDER += [0, 5, 6, 19, 24, 25]
SLOT = [ORDER.index(q) for q in range(26)]
SLANTED = [(11, 12), (14, 13), (15, 16), (18, 17)]
ROW = 8


def collide(f, flags):
    solid = (flags & 1) == 1
    open_wall = jnp.where(solid, 0.0, (flags >> 1).astype(jnp.float32))
    both = {q: f[q] + f[q + 1] for q in (*range(1, 19, 2), 20, 22, 24)}
    diff = {q: f[q] - f[q + 1] for q in (*range(1, 19, 2), 20, 22, 24)}
    density = f[0] + (
        ((both[1] + both[3]) + (both[5] + both[7]))
        + ((both[9] + both[11]) + (both[13] + both[15]))
        + both[17]
    )
    flux = [
        (diff[1] + diff[7]) + (diff[9] + diff[11]) + diff[13],
        (diff[3] + diff[7]) + (diff[15] + diff[17]) - diff[9],
        (diff[5] + diff[11]) + (diff[15] - diff[13]) - diff[17],
    ]
    inverse = 1.0 / density
    speed = [j * inverse for j in flux]
    rest = density - 1.5 * (flux[0] * speed[0] + flux[1] * speed[1] + flux[2] * speed[2])
    scaled = [4.5 * u for u in speed]

    def along(vec, values):
        total = None
        for sign, value in zip(vec, values):
            if sign == 0:
                continue
            if total is None:
                total = value
            else:
                total = total + value if sign > 0 else total - value
        return total

    post = [None] * 26
    post[0] = f[0] * (1.0 - 1.0 / tau_plus) + rest * (1.0 / (3.0 * tau_plus))
    for q in range(1, 19, 2):
        vec, weight = VELOCITY[q], FLOW_WEIGHT[q]
        j = along(vec, flux)
        even = j * along(vec, scaled) + rest
        dplus = both[q] * (0.5 / tau_plus) - even * (weight / tau_plus)
        dminus = diff[q] * (0.5 / tau_minus) - j * (3.0 * weight / tau_minus)
        post[q] = (f[q] - dplus) - dminus
        post[q + 1] = (f[q + 1] - dplus) + dminus
    conc = f[19] + ((both[20] + both[22]) + both[24])
    post[19] = f[19] * (1.0 - 1.0 / salt_plus) + conc * (0.25 / salt_plus)
    even = conc * (0.125 / salt_plus)
    for a in range(3):
        q = 20 + 2 * a
        dplus = both[q] * (0.5 / salt_plus) - even
        dminus = (diff[q] - conc * speed[a]) * (0.5 / salt_minus)
        post[q] = (f[q] - dplus) - dminus
        post[q + 1] = (f[q + 1] - dplus) + dminus
    for first in (*range(1, 19, 2), 20, 22, 24):
        post[first] = jnp.where(solid, f[first + 1], post[first])
        post[first + 1] = jnp.where(solid, f[first], post[first + 1])
    post[0] = jnp.where(solid, f[0], post[0])
    post[19] = jnp.where(solid, f[19], post[19])
    flow_loss = density * ((0.27 - 0.09 * conc) * open_wall)
    salt_loss = (0.02 * conc) * open_wall
    return post, flow_loss, salt_loss


def kernel(
    sizes, pops, flags, out, state, flag, fields, post, enter, load_sem, out_sem, send_sem, recv_sem
):
    nx, ny = sizes
    n_tiles = ny // 8
    nz = state.shape[-1]
    last = nx - 1
    below, above = ROW - 1, ROW + ny

    size_x, size_y = lax.axis_size("gx"), lax.axis_size("gy")
    gx, gy = lax.axis_index("gx"), lax.axis_index("gy")
    odd = lax.rem(gx, 2)
    far = lax.rem(gx + size_x - 1 + 2 * odd, size_x)
    near = lax.rem(gx + 1 + size_x - 2 * odd, size_x)
    other = lax.rem(gy + 1, size_y)
    ahead = gx < 2
    far_x, near_x = odd * last, (1 - odd) * last

    def tile(k):
        return k + gy * (n_tiles - 1 - 2 * k)

    def load(i, x, n):
        return pltpu.make_async_copy(
            pops.at[:, pl.ds(x, n)], state.at[:, pl.ds(x, n)], load_sem.at[i]
        )

    flag_load = pltpu.make_async_copy(flags, flag, load_sem.at[3])
    loads = [load(0, far_x, 1), load(1, near_x, 1), load(2, 1, nx - 2)]
    flag_load.start()
    for item in loads:
        item.start()

    barrier = pltpu.get_barrier_semaphore()
    partners = [(far, gy), (near, gy), (gx, other), (far, other), (near, other)]
    for px, py in partners:
        pl.semaphore_signal(
            barrier, inc=1, device_id={"gx": px, "gy": py}, device_id_type=MESH
        )

    lane = lax.broadcasted_iota(jnp.int32, (8, nz), 1)
    floor, ceiling = lane == 0, lane == nz - 1

    def copies(s):
        buf = post.at[s]

        def copy(i, src, dst, px, py):
            return pltpu.make_async_remote_copy(
                src_ref=buf.at[src],
                dst_ref=buf.at[dst],
                send_sem=send_sem.at[s, i],
                recv_sem=recv_sem.at[s, i],
                device_id={"gx": px, "gy": py},
                device_id_type=MESH,
            )

        def at(slot, n, x, nxs, row, rows=1):
            return (pl.ds(slot, n), pl.ds(x, nxs), pl.ds(row, rows))

        top = ROW + ny - 1

        def side(i, positive, x, there):
            group, halo = 10 - 10 * positive, (1 - positive) * (nx + 1)
            up, down = group + 5 * positive, group + 5 * (1 - positive)
            first, final = gy * up + (1 - gy) * down, gy * down + (1 - gy) * up
            begin, end = ROW + gy * (ny - 1), ROW + (1 - gy) * (ny - 1)
            beyond, before = ROW + ny - gy * (ny + 1), ROW - 1 + gy * (ny + 1)
            parts = []
            for k in range(n_tiles):
                row = pl.multiple_of(ROW + 8 * tile(k), 8)
                parts.append(
                    copy(i + k, at(group, 6, x + 1, 1, row, 8), at(group, 6, halo, 1, row, 8), there, gy)
                )
            i += n_tiles
            corners = [
                copy(i, at(first, 1, x + 1, 1, begin), at(first, 1, halo, 1, beyond), there, other),
                copy(i + 1, at(final, 1, x + 1, 1, end), at(final, 1, halo, 1, before), there, other),
            ]
            return parts, corners

        n_side = n_tiles + 2
        to_far = side(0, odd, far_x, far)
        to_near = side(n_side, 1 - odd, near_x, near)
        i = 2 * n_side
        to_other = [
            copy(i, at(5, 6, 1, nx, top), at(5, 6, 1, nx, below), gx, other),
            copy(i + 1, at(15, 5, 1, nx, ROW), at(15, 5, 1, nx, above), gx, other),
            copy(i + 2, at(0, 1, 1, nx, ROW), at(0, 1, 1, nx, above), gx, other),
        ]
        return to_far, to_near, to_other

    exchange = [copies(s) for s in range(STEPS)]

    def tile_rows(t):
        return pl.ds(pl.multiple_of(8 * t, 8), 8)

    def pull(s, x, t):
        f = []
        for q in range(26):
            ex, ey, ez = VECTORS[q]
            f.append(post[s, SLOT[q], x + (1 - ex), pl.ds(8 * t + (ROW - ey), 8), :])
        for i, (rising, falling) in enumerate(SLANTED):
            wall = enter[s, i, x, tile_rows(t), :]
            f[rising] = jnp.where(floor, wall, f[rising])
            f[falling] = jnp.where(ceiling, wall, f[falling])
        return f

    def advance(s, x, t):
        rows = tile_rows(t)
        if s == 0:
            f = [state[q, x, rows, :] for q in range(26)]
        else:
            f = pull(s - 1, x, t)
        new, flow_loss, salt_loss = collide(f, flag[x, rows, :])

        def up(value):
            return pltpu.roll(value, 1, 1)

        def down(value):
            return pltpu.roll(value, nz - 1, 1)

        for i, (rising, falling) in enumerate(SLANTED):
            wall = jnp.where(floor, new[falling], new[rising])
            enter[s, i, x, rows, :] = wall - FLOW_WEIGHT[rising] * flow_loss
            new[rising], new[falling] = up(new[rising]), down(new[falling])
        for rising, falling, loss in ((5, 6, FLOW_WEIGHT[5] * flow_loss), (24, 25, salt_loss)):
            low, high = new[falling] - loss, new[rising] - loss
            new[rising] = jnp.where(floor, low, up(new[rising]))
            new[falling] = jnp.where(ceiling, high, down(new[falling]))
        for q in range(26):
            post[s, SLOT[q], x + 1, pl.ds(pl.multiple_of(ROW + 8 * t, 8), 8), :] = new[q]

    def measure(x, t):
        f = pull(STEPS - 1, x, t)
        rows = tile_rows(t)
        fields[0, x, rows, :] = sum(f[1:19], f[0])
        for a in range(3):
            total = None
            for q in range(1, 19, 2):
                sign = VELOCITY[q][a]
                if sign:
                    term = f[q] - f[q + 1]
                    if total is None:
                        total = term if sign > 0 else -term
                    else:
                        total = total + term if sign > 0 else total - term
            fields[1 + a, x, rows, :] = total * (1.0 / speed_scale)
        fields[4, x, rows, :] = sum(f[20:], f[19])

    def planes(work, lo, hi, tiles):
        def body(x, carry):
            for t in tiles:
                work(x, t)
            return carry

        lax.fori_loop(lo, hi, body, 0)

    every = range(n_tiles)
    middle = range(1, n_tiles - 1)
    edge = (0, n_tiles - 1)

    def start(items):
        for item in items:
            item.start()

    def arrive(items):
        for item in items:
            item.wait_recv()

    def send(side, k):
        parts, corners = side
        if k == 0:
            corners[0].start()
        parts[k].start()
        if k == n_tiles - 1:
            corners[1].start()

    def receive(side, k):
        parts, corners = side
        if k == 0:
            arrive([corners[0], parts[0]])
        if k + 1 < n_tiles:
            arrive([parts[k + 1]])
        else:
            arrive([corners[1]])

    def store(i, x, n):
        item = pltpu.make_async_copy(
            fields.at[:, pl.ds(x, n)], out.at[:, pl.ds(x, n)], out_sem.at[i]
        )
        item.start()
        return item

    work = functools.partial(advance, 0)
    flag_load.wait()
    loads[0].wait()
    for k in every:
        work(far_x, tile(k))
        if k == 0:
            @pl.when(ahead)
            def _():
                loads[2].wait()
                planes(work, 1, last, every)

            pl.semaphore_wait(barrier, len(partners))
        send(exchange[0][0], k)
    loads[1].wait()
    for k in every:
        work(near_x, tile(k))
        send(exchange[0][1], k)

    @pl.when(jnp.logical_not(ahead))
    def _():
        loads[2].wait()
        planes(work, 1, last, every)

    start(exchange[0][2])

    for s in range(1, STEPS):
        work = functools.partial(advance, s)
        to_far, to_near, to_other = exchange[s - 1]
        planes(work, 1, last, middle)
        arrive(to_other)
        planes(work, 1, last, edge)
        for k in every:
            receive(to_far, k)
            work(far_x, tile(k))
            send(exchange[s][0], k)
            receive(to_near, k)
            work(near_x, tile(k))
            send(exchange[s][1], k)
        start(exchange[s][2])

    to_far, to_near, to_other = exchange[STEPS - 1]
    planes(measure, 1, last, middle)
    arrive(to_other)
    planes(measure, 1, last, edge)
    stores = [store(0, 1, nx - 2)]
    for k in every:
        receive(to_near, k)
        measure(near_x, tile(k))
    stores.append(store(1, near_x, 1))
    for k in every:
        receive(to_far, k)
        measure(far_x, tile(k))
    stores.append(store(2, far_x, 1))

    for to_far, to_near, to_other in exchange:
        for item in (*to_far[0], *to_far[1], *to_near[0], *to_near[1], *to_other):
            item.wait_send()
    for item in stores:
        item.wait()


def per_device(populations, cell_flags):
    _, nx, ny, nz = populations.shape
    return pl.pallas_call(
        functools.partial(kernel, (nx, ny)),
        out_shape=jax.ShapeDtypeStruct((5, nx, ny, nz), jnp.float32),
        in_specs=[pl.BlockSpec(memory_space=pltpu.HBM)] * 2,
        out_specs=pl.BlockSpec(memory_space=pltpu.HBM),
        scratch_shapes=[
            pltpu.VMEM((26, nx, ny, nz), jnp.float32),
            pltpu.VMEM((nx, ny, nz), jnp.int32),
            pltpu.VMEM((5, nx, ny, nz), jnp.float32),
            pltpu.VMEM((STEPS, 26, nx + 2, ny + 2 * ROW, nz), jnp.float32),
            pltpu.VMEM((STEPS, 4, nx, ny, nz), jnp.float32),
            pltpu.SemaphoreType.DMA((4,)),
            pltpu.SemaphoreType.DMA((3,)),
            pltpu.SemaphoreType.DMA((STEPS, 2 * (ny // 8 + 2) + 3)),
            pltpu.SemaphoreType.DMA((STEPS, 2 * (ny // 8 + 2) + 3)),
        ],
        compiler_params=pltpu.CompilerParams(
            collective_id=0, has_side_effects=True, vmem_limit_bytes=52 * 2**20
        ),
        cost_estimate=pl.CostEstimate(
            flops=900 * nx * ny * nz, bytes_accessed=128 * nx * ny * nz, transcendentals=0
        ),
    )(populations, pltpu.with_memory_space_constraint(cell_flags, pltpu.HBM))


def solution(mesh):
    return jax.shard_map(
        per_device,
        mesh=mesh,
        in_specs=(P("seg", "gx", "gy", None), P("gx", "gy", "seg")),
        out_specs=P("seg", "gx", "gy", None),
        check_vma=False,
    )
```
